32 devices in a mesh: grp: 2 (over y), row: 4 (over z), col: 2 (over x), rep: 2 (over core).
Axes of the slice: x: 2, y: 2, z: 4, core: 2. Of those that a mesh axis runs over, the one named last changes fastest.
Arguments:
- integrals: bfloat16 [512, 32, 512], P(None, ('grp', 'col', 'rep'), 'row'), parts along dimension 1, may hold values from -6 to 6
- occupied: bfloat16 [1024, 512], P(('grp', 'row', 'col')), parts along dimension 0, may hold values from -0.25 to 0.25
- virtual: bfloat16 [1024, 512], P(('grp', 'row', 'col')), parts along dimension 0, may hold values from -0.25 to 0.25
- pair_mask: int32 [4, 4], replicated, may hold values from 0 to 1, as said below
- occ_mask: int32 [4, 4], replicated, may hold values from 0 to 1, as said below
- virt_mask: int32 [4, 4], replicated, may hold values from 0 to 1, as said below
- block_sizes: int32 [4], replicated, may hold values from 64 to 128, as said below
Outputs:
- product: bfloat16 [512, 32, 512], P('row', ('grp', 'col', 'rep')), parts along dimension 1
The draws below stay inside these ranges and needn't reach their ends.
There are 2 independent parts, one for each index of `grp`. The reference program is written for one: setup_inputs(seed, part) draws one part's arguments, and reference() takes and returns one part's arrays. A program takes and returns all parts, laid end to end along the dimension named above; an argument that names none is the same for every part. Nothing has to cross between parts.
Inputs may be any that keep to these rules, and one draw needn't show every extreme that they name: `pair_mask`: each column holds between 1 and 2 ones; some column holds exactly 2. `occ_mask`: diagonal blocks are 1. `virt_mask`: diagonal blocks are 1. `block_sizes`: some block holds exactly 128 functions and some other block exactly 64.
All inputs are finite; a program needn't handle non-finite values.
Results may differ from the reference program's by a relative error of at most 0.005.
Values may be sent and summed in bfloat16 or wider, within the bound.
A program may use at most 64 MiB of HBM per device.

```python
import jax
import jax.numpy as jnp
from jax import lax

BS = 128
NAO = 512
PS = 16
NB = 4
KMAX = 2


def density_pattern(key):
    drawn = jax.random.randint(key, (NB, NB), 0, 1000) < 600
    pattern = drawn | jnp.eye(NB, dtype=bool)
    pattern = pattern.at[0, NB - 1].set(False)
    return pattern.astype(jnp.int32)


def draw_pair_mask(key, part):
    key = jax.random.fold_in(key, 17)
    key = jax.random.fold_in(key, 1701)
    key_counts, key_pick, key_scores = jax.random.split(key, 3)
    counts = jax.random.randint(key_counts, (NB,), 1, KMAX + 1)
    chosen = jax.random.randint(key_pick, (), 0, NB)
    counts = jnp.where(jnp.arange(NB) == chosen, KMAX, counts)
    scores = jax.random.randint(key_scores, (NB, NB), 0, 1000000) * NB + jnp.arange(NB)[:, None]
    ranks = jnp.argsort(jnp.argsort(scores, axis=0), axis=0)
    return (ranks < counts[None, :]).astype(jnp.int32)


def draw_occ_mask(key, part):
    key = jax.random.fold_in(key, 23)
    return density_pattern(jax.random.fold_in(key, 2311))


def draw_virt_mask(key, part):
    key = jax.random.fold_in(key, 29)
    return density_pattern(jax.random.fold_in(key, 2927))


def draw_block_sizes(key, part):
    key = jax.random.fold_in(key, 31)
    key_sizes, key_pick = jax.random.split(key)
    block_lens = jax.random.randint(key_sizes, (NB,), BS // 2, BS + 1)
    order = jax.random.permutation(key_pick, NB)
    block_lens = jnp.where(jnp.arange(NB) == order[0], BS, block_lens)
    block_lens = jnp.where(jnp.arange(NB) == order[1], BS // 2, block_lens)
    return block_lens.astype(jnp.int32)


def block_levels(key, extent, shards, least, high):
    factor_of = 1.0
    for dim, shards_of in shards:
        draws = jax.random.uniform(jax.random.fold_in(jax.random.fold_in(key, 6), dim), (shards_of,), jnp.float32, least / len(shards), high / len(shards))
        factor_of = factor_of * jnp.repeat(jnp.exp(draws), extent[dim] // shards_of).reshape((-1,) + (1,) * (len(extent) - 1 - dim))
    return factor_of


def bell_draw(stream_key, shape, spread, limit, shards=(), held_as=jnp.bfloat16):
    gain = block_levels(stream_key, shape, shards, -0.22, 0.18) if shards else 1.0
    values = jax.random.normal(stream_key, shape, jnp.float32) * spread * gain
    return jnp.minimum(jnp.maximum(values, -limit), limit).astype(held_as)


def setup_inputs(seed: int = 0, part: int = 0) -> dict:
    seeds = jax.random.split(jax.random.key(seed), 8)
    part_splits = jax.random.split(jax.random.fold_in(seeds[7], part), 8)
    integrals = bell_draw(part_splits[0], (NAO, PS, NAO), 1.0, 6.0, ((1, 4), (2, 4)))
    occupied = bell_draw(part_splits[1], (NAO, NAO), NAO ** -0.5, 0.25, ((0, 8),))
    virtual = bell_draw(part_splits[2], (NAO, NAO), NAO ** -0.5, 0.25, ((0, 8),))
    pair_mask = draw_pair_mask(jax.random.fold_in(seeds[7], 71), part)
    occ_mask = draw_occ_mask(jax.random.fold_in(seeds[7], 71), part)
    virt_mask = draw_virt_mask(jax.random.fold_in(seeds[7], 71), part)
    block_sizes = draw_block_sizes(jax.random.fold_in(seeds[7], 71), part)
    return {"integrals": integrals, "occupied": occupied, "virtual": virtual, "pair_mask": pair_mask, "occ_mask": occ_mask, "virt_mask": virt_mask, "block_sizes": block_sizes}


def expand_blocks(block_mask):
    widened = jnp.repeat(block_mask.astype(jnp.float32), BS, axis=0)
    return jnp.repeat(widened, BS, axis=1)


def live_vector(block_sizes):
    within = lax.broadcasted_iota(jnp.int32, (NB, BS), 1)
    return (within < block_sizes[:, None]).astype(jnp.float32).reshape(NAO)


def reference(integrals, occupied, virtual, pair_mask, occ_mask, virt_mask, block_sizes):
    active = live_vector(block_sizes)
    both_ends = active[:, None] * active[None, :]
    occ_eff = occupied * (expand_blocks(occ_mask) * both_ends).astype(jnp.bfloat16)
    virt_eff = virtual * (expand_blocks(virt_mask) * both_ends).astype(jnp.bfloat16)
    pair_factor = (expand_blocks(pair_mask) * both_ends).astype(jnp.bfloat16)
    tensor = integrals * pair_factor[:, None, :]

    def one_function(aux_index):
        column = lax.dynamic_index_in_dim(tensor, aux_index, 1, keepdims=False)
        halfway = jnp.dot(occ_eff, column, preferred_element_type=jnp.float32).astype(jnp.bfloat16)
        return jnp.dot(halfway, virt_eff, preferred_element_type=jnp.float32).astype(jnp.bfloat16)

    stacked = lax.map(one_function, jnp.arange(PS, dtype=jnp.int32))
    return jnp.transpose(stacked, (1, 0, 2))
```

```python
import functools

import jax
import jax.numpy as jnp
from jax import lax
from jax.experimental import pallas as pl
from jax.experimental.pallas import tpu as pltpu
from jax.sharding import PartitionSpec as P

MESH = pl.DeviceIdType.MESH
F32 = jnp.float32
BF16 = jnp.bfloat16


def loop(count, body):
    if count <= 4:
        for step in range(count):
            body(step)
    else:
        lax.fori_loop(0, count, lambda step, _: (body(step), 0)[1], 0)


def kernel(
    dims,
    pair_ref,
    occ_mask_ref,
    virt_mask_ref,
    sizes_ref,
    tensor_ref,
    occ_ref,
    virt_ref,
    out_ref,
    masked,
    packed,
    occ_all,
    virt_all,
    chosen,
    half_out,
    half_in,
    total,
    occ_send,
    occ_recv,
    pass_send,
    pass_recv,
    v1_send,
    v1_recv,
    v2_send,
    v2_recv,
    v3_send,
    v3_recv,
    h_send,
    h_recv,
):
    rows, cols, blocks, most, bs, chunk, aux = dims
    r = lax.axis_index("row")
    c = lax.axis_index("col")
    rep = lax.axis_index("rep")
    other = 1 - rep
    keep = most // 2
    wide = blocks // 2
    keep_own, keep_other = pl.ds(rep * keep, keep), pl.ds(other * keep, keep)
    wide_own, wide_other = pl.ds(rep * wide, wide), pl.ds(other * wide, wide)

    def row_at(step):
        return lax.rem(r + step, rows)

    def row_from(step):
        return lax.rem(r + rows - step, rows)

    def col_at(step):
        return lax.rem(c + step, cols)

    def col_from(step):
        return lax.rem(c + cols - step, cols)

    barrier = pltpu.get_barrier_semaphore()

    def greet(step):
        pl.semaphore_signal(
            barrier,
            inc=1,
            device_id={"row": row_at(step // cols), "col": col_at(step % cols)},
            device_id_type=MESH,
        )

    if rows * cols <= 8:
        for step in range(1, rows * cols):
            greet(step)
    else:
        lax.fori_loop(1, rows * cols, lambda step, _: (greet(step), 0)[1], 0)
    pl.semaphore_signal(barrier, inc=1, device_id={"rep": other}, device_id_type=MESH)

    def pick(column, place):
        weights, seen = [], jnp.int32(0)
        for block in range(blocks):
            here = (pair_ref[block, column] != 0).astype(jnp.int32)
            weights.append((here * (seen == place).astype(jnp.int32)).astype(F32))
            seen = seen + here
        return weights

    lane = lax.broadcasted_iota(jnp.int32, (chunk, bs), 1)
    in_block = c * chunk + lax.broadcasted_iota(jnp.int32, (chunk, bs), 0)
    row_live = (in_block < sizes_ref[r]).astype(F32)

    for block in range(blocks):
        values = occ_ref[:, block * bs : (block + 1) * bs].astype(F32)
        live = (lane < sizes_ref[block]).astype(F32)
        weight = occ_mask_ref[r, block].astype(F32)
        masked[block] = values * (live * row_live * weight)

    def pack(step):
        for j in range(keep):
            weights = pick(row_at(step), rep * keep + j)
            packed[step, j] = sum(masked[b] * weights[b] for b in range(blocks)).astype(BF16)

    loop(rows, pack)
    occ_all[r, c, keep_own] = packed[0]
    for place in range(wide):
        block = rep * wide + place
        values = virt_ref[:, pl.ds(pl.multiple_of(block * bs, bs), bs)].astype(F32)
        live = (lane < sizes_ref[block]).astype(F32)
        weight = virt_mask_ref[r, block].astype(F32)
        virt_all[c, r, block] = (values * (live * row_live * weight)).astype(BF16)

    pl.semaphore_wait(barrier, rows * cols)

    def occ_copy(step, side, source_r, source_c):
        return pltpu.make_async_remote_copy(
            src_ref=packed.at[step],
            dst_ref=occ_all.at[source_r, source_c, keep_own],
            send_sem=occ_send.at[step, side],
            recv_sem=occ_recv.at[step, side],
            device_id={"row": row_at(step), "col": col_at(side)},
            device_id_type=MESH,
        )

    def send_occ(step):
        for side in range(cols):
            if isinstance(step, int) and step == 0 and side == 0:
                continue
            occ_copy(step, side, r, c).start()

    def send_v1(step):
        v1_copy(step, r).start()

    def v1_copy(step, source_r):
        return pltpu.make_async_remote_copy(
            src_ref=virt_all.at[c, source_r, wide_own],
            dst_ref=virt_all.at[c, source_r, wide_own],
            send_sem=v1_send.at[step],
            recv_sem=v1_recv.at[step],
            device_id={"row": row_at(step)},
            device_id_type=MESH,
        )

    def v2_copy(side, source_c):
        return pltpu.make_async_remote_copy(
            src_ref=virt_all.at[source_c, :, wide_own],
            dst_ref=virt_all.at[source_c, :, wide_own],
            send_sem=v2_send.at[side],
            recv_sem=v2_recv.at[side],
            device_id={"col": col_at(side)},
            device_id_type=MESH,
        )

    def v3_copy(part):
        return pltpu.make_async_remote_copy(
            src_ref=virt_all.at[:, :, part],
            dst_ref=virt_all.at[:, :, part],
            send_sem=v3_send.at[0],
            recv_sem=v3_recv.at[0],
            device_id={"rep": other},
            device_id_type=MESH,
        )

    def pass_copy(block, part):
        return pltpu.make_async_remote_copy(
            src_ref=occ_all.at[block, :, part],
            dst_ref=occ_all.at[block, :, part],
            send_sem=pass_send.at[block],
            recv_sem=pass_recv.at[block],
            device_id={"rep": other},
            device_id_type=MESH,
        )

    def half_copy(step):
        return pltpu.make_async_remote_copy(
            src_ref=half_out.at[step],
            dst_ref=half_in.at[step],
            send_sem=h_send.at[step],
            recv_sem=h_recv.at[step],
            device_id={"row": row_at(step)},
            device_id_type=MESH,
        )

    far = rows - 1
    loop(far, lambda step: send_occ(step + 1))
    send_occ(0)
    loop(far, lambda step: send_v1(step + 1))

    tall = lax.broadcasted_iota(jnp.int32, (bs, bs), 0)
    across = lax.broadcasted_iota(jnp.int32, (bs, bs), 1)
    n_live = (across < sizes_ref[r]).astype(F32)
    picks = [pick(r, j) for j in range(most)]
    for p in range(aux):
        span = slice(p * bs, (p + 1) * bs)
        for j in range(most):
            terms = []
            for b in range(blocks):
                live = n_live * (tall < sizes_ref[b]).astype(F32) * picks[j][b]
                terms.append(tensor_ref[b * bs : (b + 1) * bs, span].astype(F32) * live)
            chosen[j * bs : (j + 1) * bs, span] = sum(terms).astype(BF16)

    def hand_on(step):
        source = row_from(step)
        for side in range(cols):
            if isinstance(step, int) and step == 0 and side == 0:
                continue
            occ_copy(step, side, source, col_from(side)).wait_recv()
        pass_copy(source, keep_own).start()

    loop(far, lambda step: hand_on(step + 1))
    hand_on(0)

    def first(step):
        goal = row_from(step)
        pass_copy(goal, keep_other).wait_recv()
        left = jnp.concatenate(
            [
                jnp.concatenate([occ_all[goal, side, j] for side in range(cols)], axis=0)
                for j in range(most)
            ],
            axis=1,
        )
        back = lax.rem(rows - step, rows)
        result = jnp.dot(left, chosen[...], preferred_element_type=F32).astype(BF16)
        if isinstance(step, int) and step == 0:
            half_in[0] = result
        else:
            half_out[back] = result
            half_copy(back).start()

    loop(far, lambda step: first(step + 1))
    first(0)

    loop(far, lambda step: v1_copy(step + 1, row_from(step + 1)).wait_recv())
    loop(cols - 1, lambda side: v2_copy(side + 1, c).start())
    loop(cols - 1, lambda side: v2_copy(side + 1, col_from(side + 1)).wait_recv())
    v3_copy(wide_own).start()
    v3_copy(wide_other).wait_recv()

    def second(step):
        source = row_from(step)
        right = jnp.concatenate(
            [
                jnp.concatenate([virt_all[side, source, block] for side in range(cols)], axis=0)
                for block in range(blocks)
            ],
            axis=1,
        )
        if not (isinstance(step, int) and step == 0):
            half_copy(step).wait_recv()
        for p in range(aux):
            term = jnp.dot(
                half_in[step, :, p * bs : (p + 1) * bs], right, preferred_element_type=F32
            )
            if isinstance(step, int) and step == 0:
                total[p] = term
            else:
                total[p] += term

    second(0)
    loop(far, lambda step: second(step + 1))
    span = blocks * bs
    for p in range(aux):
        out_ref[:, p * span : (p + 1) * span] = total[p].astype(BF16)

    def close_occ(step):
        for side in range(cols):
            if isinstance(step, int) and step == 0 and side == 0:
                continue
            occ_copy(step, side, r, c).wait_send()

    def close(step):
        close_occ(step + 1)
        v1_copy(step + 1, r).wait_send()
        half_copy(step + 1).wait_send()

    close_occ(0)
    loop(far, close)
    loop(rows, lambda block: pass_copy(block, keep_own).wait_send())
    loop(cols - 1, lambda side: v2_copy(side + 1, c).wait_send())
    v3_copy(wide_own).wait_send()


def per_device(rows, cols, integrals, occupied, virtual, pair_mask, occ_mask, virt_mask, sizes):
    total_ao, aux, ao_local = integrals.shape
    blocks = sizes.shape[0]
    bs = total_ao // blocks
    most = max(blocks // 2, 1)
    chunk = occupied.shape[0]
    dims = (rows, cols, blocks, most, bs, chunk, aux)
    smem = pl.BlockSpec(memory_space=pltpu.SMEM)
    vmem = pl.BlockSpec(memory_space=pltpu.VMEM)
    dma = pltpu.SemaphoreType.DMA
    result = pl.pallas_call(
        functools.partial(kernel, dims),
        out_shape=jax.ShapeDtypeStruct((bs, aux * total_ao), BF16),
        in_specs=[smem] * 4 + [vmem] * 3,
        out_specs=vmem,
        scratch_shapes=[
            pltpu.VMEM((blocks, chunk, bs), F32),
            pltpu.VMEM((rows, most // 2, chunk, bs), BF16),
            pltpu.VMEM((rows, cols, most, chunk, bs), BF16),
            pltpu.VMEM((cols, rows, blocks, chunk, bs), BF16),
            pltpu.VMEM((most * bs, aux * ao_local), BF16),
            pltpu.VMEM((rows, bs, aux * ao_local), BF16),
            pltpu.VMEM((rows, bs, aux * ao_local), BF16),
            pltpu.VMEM((aux, bs, total_ao), F32),
            dma((rows, cols)),
            dma((rows, cols)),
            dma((rows,)),
            dma((rows,)),
            dma((rows,)),
            dma((rows,)),
            dma((cols,)),
            dma((cols,)),
            dma((1,)),
            dma((1,)),
            dma((rows,)),
            dma((rows,)),
        ],
        compiler_params=pltpu.CompilerParams(
            collective_id=0, has_side_effects=True, vmem_limit_bytes=48 * 1024 * 1024
        ),
        name="contract",
    )(
        pair_mask,
        occ_mask,
        virt_mask,
        sizes,
        integrals.reshape(total_ao, aux * ao_local),
        occupied,
        virtual,
    )
    return result.reshape(bs, aux, total_ao)


def solution(mesh):
    in_specs = (
        P(None, ("grp", "col", "rep"), "row"),
        P(("grp", "row", "col"), None),
        P(("grp", "row", "col"), None),
        P(),
        P(),
        P(),
        P(),
    )
    out_specs = P("row", ("grp", "col", "rep"), None)
    return jax.shard_map(
        functools.partial(per_device, mesh.shape["row"], mesh.shape["col"]),
        mesh=mesh,
        in_specs=in_specs,
        out_specs=out_specs,
        check_vma=False,
    )
```

```python
import functools

import jax
import jax.numpy as jnp
from jax import lax
from jax.experimental import pallas as pl
from jax.experimental.pallas import tpu as pltpu
from jax.sharding import PartitionSpec as P

MESH = pl.DeviceIdType.MESH
F32 = jnp.float32
BF16 = jnp.bfloat16


def loop(count, body):
    if count <= 4:
        for step in range(count):
            body(step)
    else:
        lax.fori_loop(0, count, lambda step, _: (body(step), 0)[1], 0)


def kernel(
    dims,
    pair_ref,
    occ_mask_ref,
    virt_mask_ref,
    sizes_ref,
    tensor_ref,
    occ_ref,
    virt_ref,
    out_ref,
    masked,
    packed,
    occ_all,
    virt_all,
    chosen,
    half_out,
    half_in,
    total,
    occ_send,
    occ_recv,
    pass_send,
    pass_recv,
    v1_send,
    v1_recv,
    v2_send,
    v2_recv,
    v3_send,
    v3_recv,
    h_send,
    h_recv,
):
    rows, cols, blocks, most, bs, chunk, aux = dims
    r = lax.axis_index("row")
    c = lax.axis_index("col")
    rep = lax.axis_index("rep")
    other = 1 - rep
    keep = most // 2
    wide = blocks // 2
    keep_own, keep_other = pl.ds(rep * keep, keep), pl.ds(other * keep, keep)
    wide_own, wide_other = pl.ds(rep * wide, wide), pl.ds(other * wide, wide)

    def row_at(step):
        return lax.rem(r + step, rows)

    def row_from(step):
        return lax.rem(r + rows - step, rows)

    def col_at(step):
        return lax.rem(c + step, cols)

    def col_from(step):
        return lax.rem(c + cols - step, cols)

    barrier = pltpu.get_barrier_semaphore()

    def greet(step):
        pl.semaphore_signal(
            barrier,
            inc=1,
            device_id={"row": row_at(step // cols), "col": col_at(step % cols)},
            device_id_type=MESH,
        )

    if rows * cols <= 8:
        for step in range(1, rows * cols):
            greet(step)
    else:
        lax.fori_loop(1, rows * cols, lambda step, _: (greet(step), 0)[1], 0)
    pl.semaphore_signal(barrier, inc=1, device_id={"rep": other}, device_id_type=MESH)

    def pick(column, place):
        weights, seen = [], jnp.int32(0)
        for block in range(blocks):
            here = (pair_ref[block, column] != 0).astype(jnp.int32)
            weights.append((here * (seen == place).astype(jnp.int32)).astype(F32))
            seen = seen + here
        return weights

    lane = lax.broadcasted_iota(jnp.int32, (chunk, bs), 1)
    in_block = c * chunk + lax.broadcasted_iota(jnp.int32, (chunk, bs), 0)
    row_live = (in_block < sizes_ref[r]).astype(F32)

    for block in range(blocks):
        values = occ_ref[:, block * bs : (block + 1) * bs].astype(F32)
        live = (lane < sizes_ref[block]).astype(F32)
        weight = occ_mask_ref[r, block].astype(F32)
        masked[block] = values * (live * row_live * weight)

    def pack(step):
        for j in range(keep):
            weights = pick(row_at(step), rep * keep + j)
            packed[step, j] = sum(masked[b] * weights[b] for b in range(blocks)).astype(BF16)

    loop(rows, pack)
    occ_all[r, c, keep_own] = packed[0]
    for place in range(wide):
        block = rep * wide + place
        values = virt_ref[:, pl.ds(pl.multiple_of(block * bs, bs), bs)].astype(F32)
        live = (lane < sizes_ref[block]).astype(F32)
        weight = virt_mask_ref[r, block].astype(F32)
        virt_all[c, r, block] = (values * (live * row_live * weight)).astype(BF16)

    pl.semaphore_wait(barrier, rows * cols)

    def occ_copy(step, side, source_r, source_c):
        return pltpu.make_async_remote_copy(
            src_ref=packed.at[step],
            dst_ref=occ_all.at[source_r, source_c, keep_own],
            send_sem=occ_send.at[step, side],
            recv_sem=occ_recv.at[step, side],
            device_id={"row": row_at(step), "col": col_at(side)},
            device_id_type=MESH,
        )

    def send_occ(step):
        for side in range(cols):
            if isinstance(step, int) and step == 0 and side == 0:
                continue
            occ_copy(step, side, r, c).start()

    def send_v1(step):
        v1_copy(step, r).start()

    def v1_copy(step, source_r):
        return pltpu.make_async_remote_copy(
            src_ref=virt_all.at[c, source_r, wide_own],
            dst_ref=virt_all.at[c, source_r, wide_own],
            send_sem=v1_send.at[step],
            recv_sem=v1_recv.at[step],
            device_id={"row": row_at(step)},
            device_id_type=MESH,
        )

    def v2_copy(side, source_c):
        return pltpu.make_async_remote_copy(
            src_ref=virt_all.at[source_c, :, wide_own],
            dst_ref=virt_all.at[source_c, :, wide_own],
            send_sem=v2_send.at[side],
            recv_sem=v2_recv.at[side],
            device_id={"col": col_at(side)},
            device_id_type=MESH,
        )

    def v3_copy(part):
        return pltpu.make_async_remote_copy(
            src_ref=virt_all.at[:, :, part],
            dst_ref=virt_all.at[:, :, part],
            send_sem=v3_send.at[0],
            recv_sem=v3_recv.at[0],
            device_id={"rep": other},
            device_id_type=MESH,
        )

    def pass_copy(block, part):
        return pltpu.make_async_remote_copy(
            src_ref=occ_all.at[block, :, part],
            dst_ref=occ_all.at[block, :, part],
            send_sem=pass_send.at[block],
            recv_sem=pass_recv.at[block],
            device_id={"rep": other},
            device_id_type=MESH,
        )

    def half_copy(step):
        return pltpu.make_async_remote_copy(
            src_ref=half_out.at[step],
            dst_ref=half_in.at[step],
            send_sem=h_send.at[step],
            recv_sem=h_recv.at[step],
            device_id={"row": row_at(step)},
            device_id_type=MESH,
        )

    far = rows - 1
    loop(far, lambda step: send_occ(step + 1))
    send_occ(0)
    loop(far, lambda step: send_v1(step + 1))

    tall = lax.broadcasted_iota(jnp.int32, (bs, bs), 0)
    across = lax.broadcasted_iota(jnp.int32, (bs, bs), 1)
    n_live = (across < sizes_ref[r]).astype(F32)
    picks = [pick(r, j) for j in range(most)]
    for p in range(aux):
        span = slice(p * bs, (p + 1) * bs)
        for j in range(most):
            terms = []
            for b in range(blocks):
                live = n_live * (tall < sizes_ref[b]).astype(F32) * picks[j][b]
                terms.append(tensor_ref[b * bs : (b + 1) * bs, span].astype(F32) * live)
            chosen[j * bs : (j + 1) * bs, span] = sum(terms).astype(BF16)

    def hand_on(step):
        source = row_from(step)
        for side in range(cols):
            if isinstance(step, int) and step == 0 and side == 0:
                continue
            occ_copy(step, side, source, col_from(side)).wait_recv()
        pass_copy(source, keep_own).start()

    loop(far, lambda step: hand_on(step + 1))
    hand_on(0)

    def first(step):
        goal = row_from(step)
        pass_copy(goal, keep_other).wait_recv()
        left = jnp.concatenate(
            [
                jnp.concatenate([occ_all[goal, side, j] for side in range(cols)], axis=0)
                for j in range(most)
            ],
            axis=1,
        )
        back = (rows - step) % rows
        result = jnp.dot(left, chosen[...], preferred_element_type=F32).astype(BF16)
        if isinstance(step, int) and step == 0:
            half_in[0] = result
        else:
            half_out[back] = result
            half_copy(back).start()

    loop(far, lambda step: first(step + 1))
    first(0)

    loop(far, lambda step: v1_copy(step + 1, row_from(step + 1)).wait_recv())
    loop(cols - 1, lambda side: v2_copy(side + 1, c).start())
    loop(cols - 1, lambda side: v2_copy(side + 1, col_from(side + 1)).wait_recv())
    v3_copy(wide_own).start()
    v3_copy(wide_other).wait_recv()

    def second(step):
        source = row_from(step)
        right = jnp.concatenate(
            [
                jnp.concatenate([virt_all[side, source, block] for side in range(cols)], axis=0)
                for block in range(blocks)
            ],
            axis=1,
        )
        if not (isinstance(step, int) and step == 0):
            half_copy(step).wait_recv()
        for p in range(aux):
            term = jnp.dot(
                half_in[step, :, p * bs : (p + 1) * bs], right, preferred_element_type=F32
            )
            if isinstance(step, int) and step == 0:
                total[p] = term
            else:
                total[p] += term

    second(0)
    loop(far, lambda step: second(step + 1))
    span = blocks * bs
    for p in range(aux):
        out_ref[:, p * span : (p + 1) * span] = total[p].astype(BF16)

    def close_occ(step):
        for side in range(cols):
            if isinstance(step, int) and step == 0 and side == 0:
                continue
            occ_copy(step, side, r, c).wait_send()

    def close(step):
        close_occ(step + 1)
        v1_copy(step + 1, r).wait_send()
        half_copy(step + 1).wait_send()

    close_occ(0)
    loop(far, close)
    loop(rows, lambda block: pass_copy(block, keep_own).wait_send())
    loop(cols - 1, lambda side: v2_copy(side + 1, c).wait_send())
    v3_copy(wide_own).wait_send()


def kernel_four(
    dims,
    pair_hbm,
    occ_mask_hbm,
    virt_mask_hbm,
    sizes_hbm,
    tensor_hbm,
    occ_hbm,
    virt_hbm,
    out_ref,
    masked,
    packed,
    occ_in,
    virt_all,
    chosen,
    half_out,
    half_in,
    total,
    occ_send,
    occ_recv,
    pass_send,
    pass_recv,
    h_send,
    h_recv,
    v1_send,
    v1_recv,
    v2_send,
    v2_recv,
    v3_send,
    v3_recv,
    weave,
    loaded,
    occ_ref,
    virt_ref,
    pair_ref,
    occ_mask_ref,
    virt_mask_ref,
    sizes_ref,
    load_sem,
):
    rows, cols, blocks, most, bs, chunk, aux = dims
    r = lax.axis_index("row")
    c = lax.axis_index("col")
    rep = lax.axis_index("rep")
    other = 1 - rep
    upper = r // 2
    near = r + 1 - 2 * (r % 2)
    across = 2 - upper
    far = 3 - 3 * upper
    outer_int = 1 - (r + upper) % 2
    keep = most // 2
    wide = blocks // 2
    keep_own = pl.ds(rep * keep, keep)
    keep_other = pl.ds(other * keep, keep)
    wide_own = pl.ds(rep * wide, wide)
    wide_other = pl.ds(other * wide, wide)
    OWN, NEAR, ACROSS, FAR = range(4)
    mine = ACROSS + outer_int
    rows_of = (r, near, across, far)
    names = (OWN, NEAR, ACROSS, FAR)
    slot_there = (OWN, NEAR, mine, mine)

    barrier = pltpu.get_barrier_semaphore()
    for step in range(1, rows * cols):
        pl.semaphore_signal(
            barrier,
            inc=1,
            device_id={"row": (r + step // cols) % rows, "col": (c + step) % cols},
            device_id_type=MESH,
        )
    pl.semaphore_signal(barrier, inc=1, device_id={"rep": other}, device_id_type=MESH)
    pairs = (
        (pair_hbm, pair_ref),
        (occ_mask_hbm, occ_mask_ref),
        (sizes_hbm, sizes_ref),
        (occ_hbm, occ_ref),
        (virt_mask_hbm, virt_mask_ref),
        (virt_hbm, virt_ref),
        (tensor_hbm, loaded),
    )
    loads = [
        pltpu.make_async_copy(src, dst, load_sem.at[i]) for i, (src, dst) in enumerate(pairs)
    ]
    for load in loads:
        load.start()
    for load in loads[:4]:
        load.wait()

    def pick(column, place):
        weights, seen = [], jnp.int32(0)
        for block in range(blocks):
            here = (pair_ref[block, column] != 0).astype(jnp.int32)
            weights.append((here * (seen == place).astype(jnp.int32)).astype(F32))
            seen = seen + here
        return weights

    lane = lax.broadcasted_iota(jnp.int32, (chunk, bs), 1)
    in_block = c * chunk + lax.broadcasted_iota(jnp.int32, (chunk, bs), 0)
    row_live = (in_block < sizes_ref[r]).astype(F32)
    for block in range(blocks):
        values = occ_ref[:, block * bs : (block + 1) * bs].astype(F32)
        live = (lane < sizes_ref[block]).astype(F32)
        weight = occ_mask_ref[r, block].astype(F32)
        masked[block] = values * (live * row_live * weight)

    def pack(goal):
        slabs = []
        for j in range(keep):
            weights = pick(goal, rep * keep + j)
            slabs.append(sum(masked[b] * weights[b] for b in range(blocks)).astype(BF16))
        return jnp.stack(slabs)

    for slot in (NEAR, ACROSS, FAR):
        packed[slot - 1] = pack(rows_of[slot])
    occ_in[OWN, c, keep_own] = pack(r)
    for load in loads[4:6]:
        load.wait()
    for place in range(wide):
        block = rep * wide + place
        values = virt_ref[:, pl.ds(pl.multiple_of(block * bs, bs), bs)].astype(F32)
        live = (lane < sizes_ref[block]).astype(F32)
        weight = virt_mask_ref[r, block].astype(F32)
        virt_all[c, r, block] = (values * (live * row_live * weight)).astype(BF16)

    def send(src, dst, send_sem, recv_sem, **place):
        return pltpu.make_async_remote_copy(
            src_ref=src,
            dst_ref=dst,
            send_sem=send_sem,
            recv_sem=recv_sem,
            device_id=place,
            device_id_type=MESH,
        )

    def occ_copy(slot, side, there):
        column = c if side == 0 else 1 - c
        return send(
            occ_in.at[OWN, c, keep_own] if slot == OWN else packed.at[slot - 1],
            occ_in.at[there, c, keep_own],
            occ_send.at[slot, side],
            occ_recv.at[there, side],
            row=rows_of[slot],
            col=column,
        )

    def pass_copy(slot, part):
        slab = occ_in.at[slot, :, part]
        return send(slab, slab, pass_send.at[slot], pass_recv.at[slot], rep=other)

    def half_copy(slot, there):
        return send(
            half_out.at[slot - 1],
            half_in.at[there],
            h_send.at[slot],
            h_recv.at[there],
            row=rows_of[slot],
        )

    def virt_copy(slot, there):
        slab = virt_all.at[c, r, wide_own]
        return send(slab, slab, v1_send.at[slot], v1_recv.at[there], row=rows_of[slot])

    def v2_copy(column):
        slab = virt_all.at[column, :, wide_own]
        return send(slab, slab, v2_send.at[0], v2_recv.at[0], col=1 - c)

    def v3_copy(part):
        slab = virt_all.at[:, :, part]
        return send(slab, slab, v3_send.at[0], v3_recv.at[0], rep=other)

    pl.semaphore_wait(barrier, rows * cols)

    sends = [(FAR, 0), (ACROSS, 0), (FAR, 1), (ACROSS, 1), (NEAR, 0), (NEAR, 1), (OWN, 1)]
    for slot, side in sends:
        occ_copy(slot, side, slot_there[slot]).start()
    virt_copy(NEAR, NEAR).start()
    virt_copy(ACROSS, mine).start()
    virt_copy(FAR, mine).start()

    loads[6].wait()
    span = bs * aux
    gap = lax.broadcasted_iota(jnp.int32, (bs, span), 1) - aux * lax.broadcasted_iota(
        jnp.int32, (bs, span), 0
    )
    order = jnp.concatenate([(gap == p).astype(F32).astype(BF16) for p in range(aux)], axis=0)
    tall = lax.broadcasted_iota(jnp.int32, (span, bs), 0)
    n_live = (lax.broadcasted_iota(jnp.int32, (span, bs), 1) < sizes_ref[r]).astype(F32)
    lit = [
        loaded[b * span : (b + 1) * span, :]
        * (n_live * (tall < aux * sizes_ref[b]).astype(F32)).astype(BF16)
        for b in range(blocks)
    ]
    for j in range(most):
        weights = pick(r, j)
        value = sum(lit[b] * weights[b].astype(BF16) for b in range(blocks))
        turned = jnp.dot(order, value, preferred_element_type=F32).astype(BF16)
        for p in range(aux):
            chosen[j * bs : (j + 1) * bs, p * bs : (p + 1) * bs] = turned[p * bs : (p + 1) * bs]

    for slot in (OWN, NEAR, ACROSS, FAR):
        for side in range(cols):
            if slot != OWN or side:
                occ_copy(slot, side, slot).wait_recv()
        pass_copy(slot, keep_own).start()
    def halfway(slot):
        pass_copy(slot, keep_other).wait_recv()
        left = jnp.concatenate(
            [
                jnp.concatenate([occ_in[slot, side, j] for side in range(cols)], axis=0)
                for j in range(most)
            ],
            axis=1,
        )
        return jnp.dot(left, chosen[...], preferred_element_type=F32).astype(BF16)

    for slot in (FAR, ACROSS, NEAR):
        half_out[slot - 1] = halfway(slot)
        half_copy(slot, slot_there[slot]).start()
    half_in[OWN] = halfway(OWN)

    virt_copy(NEAR, NEAR).wait_recv()

    mixed = aux * blocks
    lead = span // mixed
    parts = bs // lead
    to = lax.broadcasted_iota(jnp.int32, (span, span), 0)
    come = lax.broadcasted_iota(jnp.int32, (span, span), 1)
    low = mixed.bit_length() - 1
    weave[...] = (
        (come == (to & (mixed - 1)) * lead + lax.shift_right_logical(to, low))
        .astype(F32)
        .astype(BF16)
    )
    virt_copy(ACROSS, ACROSS).wait_recv()
    virt_copy(ACROSS, FAR).wait_recv()
    v2_copy(c).start()
    v2_copy(1 - c).wait_recv()
    v3_copy(wide_own).start()
    v3_copy(wide_other).wait_recv()

    def second(slot):
        source = rows_of[slot]
        right = jnp.concatenate(
            [
                jnp.concatenate([virt_all[side, source, block] for side in range(cols)], axis=0)
                for block in range(blocks)
            ],
            axis=1,
        )
        if slot != OWN:
            half_copy(slot, slot).wait_recv()
        for p in range(aux):
            term = jnp.dot(
                half_in[slot, :, p * bs : (p + 1) * bs], right, preferred_element_type=F32
            )
            if slot == OWN:
                total[p] = term
            else:
                total[p] += term

    for slot in (OWN, NEAR, ACROSS, FAR):
        second(slot)
    for part in range(parts):
        piece = slice(part * lead, (part + 1) * lead)
        value = jnp.concatenate(
            [
                total[p, piece, t * bs : (t + 1) * bs].astype(BF16)
                for t in range(blocks)
                for p in range(aux)
            ],
            axis=0,
        )
        turned = jnp.dot(weave[...], value, preferred_element_type=F32).astype(BF16)
        out_ref[part * span : (part + 1) * span, :] = turned

    for slot, side in sends:
        occ_copy(slot, side, slot_there[slot]).wait_send()
    for slot in names:
        pass_copy(slot, keep_own).wait_send()
        if slot != OWN:
            half_copy(slot, slot_there[slot]).wait_send()
    virt_copy(NEAR, NEAR).wait_send()
    virt_copy(ACROSS, mine).wait_send()
    virt_copy(FAR, mine).wait_send()
    v2_copy(c).wait_send()
    v3_copy(wide_own).wait_send()


def call_four(dims, operands):
    rows, cols, blocks, most, bs, chunk, aux = dims
    span = aux * bs
    vmem = pl.BlockSpec(memory_space=pltpu.VMEM)
    dma = pltpu.SemaphoreType.DMA
    one, slots = dma((1,)), dma((4,))
    return pl.pallas_call(
        functools.partial(kernel_four, dims),
        out_shape=jax.ShapeDtypeStruct((bs * blocks * aux, bs), BF16),
        in_specs=[pl.BlockSpec(memory_space=pl.ANY)] * 7,
        out_specs=vmem,
        scratch_shapes=[
            pltpu.VMEM((blocks, chunk, bs), F32),
            pltpu.VMEM((3, most // 2, chunk, bs), BF16),
            pltpu.VMEM((4, cols, most, chunk, bs), BF16),
            pltpu.VMEM((cols, rows, blocks, chunk, bs), BF16),
            pltpu.VMEM((most * bs, span), BF16),
            pltpu.VMEM((3, bs, span), BF16),
            pltpu.VMEM((4, bs, span), BF16),
            pltpu.VMEM((aux, bs, blocks * bs), F32),
            dma((4, cols)),
            dma((4, cols)),
            slots,
            slots,
            slots,
            slots,
            slots,
            slots,
            one,
            one,
            one,
            one,
            pltpu.VMEM((span, span), BF16),
            pltpu.VMEM((blocks * span, bs), BF16),
            pltpu.VMEM((chunk, blocks * bs), BF16),
            pltpu.VMEM((chunk, blocks * bs), BF16),
            pltpu.SMEM((blocks, blocks), jnp.int32),
            pltpu.SMEM((blocks, blocks), jnp.int32),
            pltpu.SMEM((blocks, blocks), jnp.int32),
            pltpu.SMEM((blocks,), jnp.int32),
            dma((7,)),
        ],
        compiler_params=pltpu.CompilerParams(
            collective_id=0, has_side_effects=True, vmem_limit_bytes=60 * 1024 * 1024
        ),
        name="contract",
    )(*operands)


def per_device(rows, cols, integrals, occupied, virtual, pair_mask, occ_mask, virt_mask, sizes):
    total_ao, aux, ao_local = integrals.shape
    blocks = sizes.shape[0]
    bs = total_ao // blocks
    most = max(blocks // 2, 1)
    chunk = occupied.shape[0]
    dims = (rows, cols, blocks, most, bs, chunk, aux)
    if rows == 4 and cols == 2 and most % 2 == 0 and blocks == rows:
        flat = integrals.reshape(total_ao * aux, ao_local)
        result = call_four(
            dims, (pair_mask, occ_mask, virt_mask, sizes, flat, occupied, virtual)
        )
        result = result.reshape(bs, blocks, aux, bs).transpose(0, 2, 1, 3)
        return result.reshape(bs, aux, total_ao)
    smem = pl.BlockSpec(memory_space=pltpu.SMEM)
    vmem = pl.BlockSpec(memory_space=pltpu.VMEM)
    dma = pltpu.SemaphoreType.DMA
    result = pl.pallas_call(
        functools.partial(kernel, dims),
        out_shape=jax.ShapeDtypeStruct((bs, aux * total_ao), BF16),
        in_specs=[smem] * 4 + [vmem] * 3,
        out_specs=vmem,
        scratch_shapes=[
            pltpu.VMEM((blocks, chunk, bs), F32),
            pltpu.VMEM((rows, most // 2, chunk, bs), BF16),
            pltpu.VMEM((rows, cols, most, chunk, bs), BF16),
            pltpu.VMEM((cols, rows, blocks, chunk, bs), BF16),
            pltpu.VMEM((most * bs, aux * ao_local), BF16),
            pltpu.VMEM((rows, bs, aux * ao_local), BF16),
            pltpu.VMEM((rows, bs, aux * ao_local), BF16),
            pltpu.VMEM((aux, bs, total_ao), F32),
            dma((rows, cols)),
            dma((rows, cols)),
            dma((rows,)),
            dma((rows,)),
            dma((rows,)),
            dma((rows,)),
            dma((cols,)),
            dma((cols,)),
            dma((1,)),
            dma((1,)),
            dma((rows,)),
            dma((rows,)),
        ],
        compiler_params=pltpu.CompilerParams(
            collective_id=0, has_side_effects=True, vmem_limit_bytes=48 * 1024 * 1024
        ),
        name="contract",
    )(
        pair_mask,
        occ_mask,
        virt_mask,
        sizes,
        integrals.reshape(total_ao, aux * ao_local),
        occupied,
        virtual,
    )
    return result.reshape(bs, aux, total_ao)


def solution(mesh):
    in_specs = (
        P(None, ("grp", "col", "rep"), "row"),
        P(("grp", "row", "col"), None),
        P(("grp", "row", "col"), None),
        P(),
        P(),
        P(),
        P(),
    )
    out_specs = P("row", ("grp", "col", "rep"), None)
    return jax.shard_map(
        functools.partial(per_device, mesh.shape["row"], mesh.shape["col"]),
        mesh=mesh,
        in_specs=in_specs,
        out_specs=out_specs,
        check_vma=False,
    )
```

```python
import functools

import jax
import jax.numpy as jnp
from jax import lax
from jax.experimental import pallas as pl
from jax.experimental.pallas import tpu as pltpu
from jax.sharding import PartitionSpec as P

MESH = pl.DeviceIdType.MESH
F32 = jnp.float32
BF16 = jnp.bfloat16


def loop(count, body):
    if count <= 4:
        for step in range(count):
            body(step)
    else:
        lax.fori_loop(0, count, lambda step, _: (body(step), 0)[1], 0)


def kernel(
    dims,
    pair_ref,
    occ_mask_ref,
    virt_mask_ref,
    sizes_ref,
    tensor_ref,
    occ_ref,
    virt_ref,
    out_ref,
    masked,
    packed,
    occ_all,
    virt_all,
    chosen,
    half_out,
    half_in,
    total,
    occ_send,
    occ_recv,
    pass_send,
    pass_recv,
    v1_send,
    v1_recv,
    v2_send,
    v2_recv,
    v3_send,
    v3_recv,
    h_send,
    h_recv,
):
    rows, cols, blocks, most, bs, chunk, aux = dims
    r = lax.axis_index("row")
    c = lax.axis_index("col")
    rep = lax.axis_index("rep")
    other = 1 - rep
    keep = most // 2
    wide = blocks // 2
    keep_own, keep_other = pl.ds(rep * keep, keep), pl.ds(other * keep, keep)
    wide_own, wide_other = pl.ds(rep * wide, wide), pl.ds(other * wide, wide)

    def row_at(step):
        return lax.rem(r + step, rows)

    def row_from(step):
        return lax.rem(r + rows - step, rows)

    def col_at(step):
        return lax.rem(c + step, cols)

    def col_from(step):
        return lax.rem(c + cols - step, cols)

    barrier = pltpu.get_barrier_semaphore()

    def greet(step):
        pl.semaphore_signal(
            barrier,
            inc=1,
            device_id={"row": row_at(step // cols), "col": col_at(step % cols)},
            device_id_type=MESH,
        )

    if rows * cols <= 8:
        for step in range(1, rows * cols):
            greet(step)
    else:
        lax.fori_loop(1, rows * cols, lambda step, _: (greet(step), 0)[1], 0)
    pl.semaphore_signal(barrier, inc=1, device_id={"rep": other}, device_id_type=MESH)

    def pick(column, place):
        weights, seen = [], jnp.int32(0)
        for block in range(blocks):
            here = (pair_ref[block, column] != 0).astype(jnp.int32)
            weights.append((here * (seen == place).astype(jnp.int32)).astype(F32))
            seen = seen + here
        return weights

    lane = lax.broadcasted_iota(jnp.int32, (chunk, bs), 1)
    in_block = c * chunk + lax.broadcasted_iota(jnp.int32, (chunk, bs), 0)
    row_live = (in_block < sizes_ref[r]).astype(F32)

    for block in range(blocks):
        values = occ_ref[:, block * bs : (block + 1) * bs].astype(F32)
        live = (lane < sizes_ref[block]).astype(F32)
        weight = occ_mask_ref[r, block].astype(F32)
        masked[block] = values * (live * row_live * weight)

    def pack(step):
        for j in range(keep):
            weights = pick(row_at(step), rep * keep + j)
            packed[step, j] = sum(masked[b] * weights[b] for b in range(blocks)).astype(BF16)

    loop(rows, pack)
    occ_all[r, c, keep_own] = packed[0]
    for place in range(wide):
        block = rep * wide + place
        values = virt_ref[:, pl.ds(pl.multiple_of(block * bs, bs), bs)].astype(F32)
        live = (lane < sizes_ref[block]).astype(F32)
        weight = virt_mask_ref[r, block].astype(F32)
        virt_all[c, r, block] = (values * (live * row_live * weight)).astype(BF16)

    pl.semaphore_wait(barrier, rows * cols)

    def occ_copy(step, side, source_r, source_c):
        return pltpu.make_async_remote_copy(
            src_ref=packed.at[step],
            dst_ref=occ_all.at[source_r, source_c, keep_own],
            send_sem=occ_send.at[step, side],
            recv_sem=occ_recv.at[step, side],
            device_id={"row": row_at(step), "col": col_at(side)},
            device_id_type=MESH,
        )

    def send_occ(step):
        for side in range(cols):
            if isinstance(step, int) and step == 0 and side == 0:
                continue
            occ_copy(step, side, r, c).start()

    def send_v1(step):
        v1_copy(step, r).start()

    def v1_copy(step, source_r):
        return pltpu.make_async_remote_copy(
            src_ref=virt_all.at[c, source_r, wide_own],
            dst_ref=virt_all.at[c, source_r, wide_own],
            send_sem=v1_send.at[step],
            recv_sem=v1_recv.at[step],
            device_id={"row": row_at(step)},
            device_id_type=MESH,
        )

    def v2_copy(side, source_c):
        return pltpu.make_async_remote_copy(
            src_ref=virt_all.at[source_c, :, wide_own],
            dst_ref=virt_all.at[source_c, :, wide_own],
            send_sem=v2_send.at[side],
            recv_sem=v2_recv.at[side],
            device_id={"col": col_at(side)},
            device_id_type=MESH,
        )

    def v3_copy(part):
        return pltpu.make_async_remote_copy(
            src_ref=virt_all.at[:, :, part],
            dst_ref=virt_all.at[:, :, part],
            send_sem=v3_send.at[0],
            recv_sem=v3_recv.at[0],
            device_id={"rep": other},
            device_id_type=MESH,
        )

    def pass_copy(block, part):
        return pltpu.make_async_remote_copy(
            src_ref=occ_all.at[block, :, part],
            dst_ref=occ_all.at[block, :, part],
            send_sem=pass_send.at[block],
            recv_sem=pass_recv.at[block],
            device_id={"rep": other},
            device_id_type=MESH,
        )

    def half_copy(step):
        return pltpu.make_async_remote_copy(
            src_ref=half_out.at[step],
            dst_ref=half_in.at[step],
            send_sem=h_send.at[step],
            recv_sem=h_recv.at[step],
            device_id={"row": row_at(step)},
            device_id_type=MESH,
        )

    far = rows - 1
    loop(far, lambda step: send_occ(step + 1))
    send_occ(0)
    loop(far, lambda step: send_v1(step + 1))

    tall = lax.broadcasted_iota(jnp.int32, (bs, bs), 0)
    across = lax.broadcasted_iota(jnp.int32, (bs, bs), 1)
    n_live = (across < sizes_ref[r]).astype(F32)
    picks = [pick(r, j) for j in range(most)]
    for p in range(aux):
        span = slice(p * bs, (p + 1) * bs)
        for j in range(most):
            terms = []
            for b in range(blocks):
                live = n_live * (tall < sizes_ref[b]).astype(F32) * picks[j][b]
                terms.append(tensor_ref[b * bs : (b + 1) * bs, span].astype(F32) * live)
            chosen[j * bs : (j + 1) * bs, span] = sum(terms).astype(BF16)

    def hand_on(step):
        source = row_from(step)
        for side in range(cols):
            if isinstance(step, int) and step == 0 and side == 0:
                continue
            occ_copy(step, side, source, col_from(side)).wait_recv()
        pass_copy(source, keep_own).start()

    loop(far, lambda step: hand_on(step + 1))
    hand_on(0)

    def first(step):
        goal = row_from(step)
        pass_copy(goal, keep_other).wait_recv()
        left = jnp.concatenate(
            [
                jnp.concatenate([occ_all[goal, side, j] for side in range(cols)], axis=0)
                for j in range(most)
            ],
            axis=1,
        )
        back = (rows - step) % rows
        result = jnp.dot(left, chosen[...], preferred_element_type=F32).astype(BF16)
        if isinstance(step, int) and step == 0:
            half_in[0] = result
        else:
            half_out[back] = result
            half_copy(back).start()

    loop(far, lambda step: first(step + 1))
    first(0)

    loop(far, lambda step: v1_copy(step + 1, row_from(step + 1)).wait_recv())
    loop(cols - 1, lambda side: v2_copy(side + 1, c).start())
    loop(cols - 1, lambda side: v2_copy(side + 1, col_from(side + 1)).wait_recv())
    v3_copy(wide_own).start()
    v3_copy(wide_other).wait_recv()

    def second(step):
        source = row_from(step)
        right = jnp.concatenate(
            [
                jnp.concatenate([virt_all[side, source, block] for side in range(cols)], axis=0)
                for block in range(blocks)
            ],
            axis=1,
        )
        if not (isinstance(step, int) and step == 0):
            half_copy(step).wait_recv()
        for p in range(aux):
            term = jnp.dot(
                half_in[step, :, p * bs : (p + 1) * bs], right, preferred_element_type=F32
            )
            if isinstance(step, int) and step == 0:
                total[p] = term
            else:
                total[p] += term

    second(0)
    loop(far, lambda step: second(step + 1))
    span = blocks * bs
    for p in range(aux):
        out_ref[:, p * span : (p + 1) * span] = total[p].astype(BF16)

    def close_occ(step):
        for side in range(cols):
            if isinstance(step, int) and step == 0 and side == 0:
                continue
            occ_copy(step, side, r, c).wait_send()

    def close(step):
        close_occ(step + 1)
        v1_copy(step + 1, r).wait_send()
        half_copy(step + 1).wait_send()

    close_occ(0)
    loop(far, close)
    loop(rows, lambda block: pass_copy(block, keep_own).wait_send())
    loop(cols - 1, lambda side: v2_copy(side + 1, c).wait_send())
    v3_copy(wide_own).wait_send()


def kernel_four(
    dims,
    pair_hbm,
    occ_mask_hbm,
    virt_mask_hbm,
    sizes_hbm,
    tensor_hbm,
    occ_hbm,
    virt_hbm,
    out_ref,
    masked,
    packed,
    occ_in,
    virt_all,
    chosen,
    half_out,
    half_in,
    total,
    occ_send,
    occ_recv,
    pass_send,
    pass_recv,
    h_send,
    h_recv,
    v1_send,
    v1_recv,
    v2_send,
    v2_recv,
    v3_send,
    v3_recv,
    loaded,
    occ_ref,
    virt_ref,
    pair_ref,
    occ_mask_ref,
    virt_mask_ref,
    sizes_ref,
    load_sem,
):
    rows, cols, blocks, most, bs, chunk, aux = dims
    r = lax.axis_index("row")
    c = lax.axis_index("col")
    rep = lax.axis_index("rep")
    other = 1 - rep
    upper = r // 2
    near = r + 1 - 2 * (r % 2)
    across = 2 - upper
    far = 3 - 3 * upper
    outer_int = 1 - (r + upper) % 2
    keep = most // 2
    wide = blocks // 2
    keep_own = pl.ds(rep * keep, keep)
    keep_other = pl.ds(other * keep, keep)
    wide_own = pl.ds(rep * wide, wide)
    wide_other = pl.ds(other * wide, wide)
    OWN, NEAR, ACROSS, FAR = range(4)
    mine = ACROSS + outer_int
    rows_of = (r, near, across, far)
    names = (OWN, NEAR, ACROSS, FAR)
    slot_there = (OWN, NEAR, mine, mine)

    barrier = pltpu.get_barrier_semaphore()
    for step in range(1, rows * cols):
        pl.semaphore_signal(
            barrier,
            inc=1,
            device_id={"row": (r + step // cols) % rows, "col": (c + step) % cols},
            device_id_type=MESH,
        )
    pl.semaphore_signal(barrier, inc=1, device_id={"rep": other}, device_id_type=MESH)
    pairs = (
        (pair_hbm, pair_ref),
        (occ_mask_hbm, occ_mask_ref),
        (sizes_hbm, sizes_ref),
        (occ_hbm, occ_ref),
        (virt_mask_hbm, virt_mask_ref),
        (virt_hbm, virt_ref),
        (tensor_hbm, loaded),
    )
    loads = [
        pltpu.make_async_copy(src, dst, load_sem.at[i]) for i, (src, dst) in enumerate(pairs)
    ]
    for load in loads:
        load.start()
    for load in loads[:4]:
        load.wait()

    def pick(column, place):
        weights, seen = [], jnp.int32(0)
        for block in range(blocks):
            here = (pair_ref[block, column] != 0).astype(jnp.int32)
            weights.append((here * (seen == place).astype(jnp.int32)).astype(F32))
            seen = seen + here
        return weights

    lane = lax.broadcasted_iota(jnp.int32, (chunk, bs), 1)
    in_block = c * chunk + lax.broadcasted_iota(jnp.int32, (chunk, bs), 0)
    row_live = (in_block < sizes_ref[r]).astype(F32)
    for block in range(blocks):
        values = occ_ref[:, block * bs : (block + 1) * bs].astype(F32)
        live = (lane < sizes_ref[block]).astype(F32)
        weight = occ_mask_ref[r, block].astype(F32)
        masked[block] = values * (live * row_live * weight)

    def pack(goal):
        slabs = []
        for j in range(keep):
            weights = pick(goal, rep * keep + j)
            slabs.append(sum(masked[b] * weights[b] for b in range(blocks)).astype(BF16))
        return jnp.stack(slabs)

    for slot in (NEAR, ACROSS, FAR):
        packed[slot - 1] = pack(rows_of[slot])
    occ_in[OWN, c, keep_own] = pack(r)
    for load in loads[4:6]:
        load.wait()
    for place in range(wide):
        block = rep * wide + place
        values = virt_ref[:, pl.ds(pl.multiple_of(block * bs, bs), bs)].astype(F32)
        live = (lane < sizes_ref[block]).astype(F32)
        weight = virt_mask_ref[r, block].astype(F32)
        virt_all[c, r, block] = (values * (live * row_live * weight)).astype(BF16)

    def send(src, dst, send_sem, recv_sem, **place):
        return pltpu.make_async_remote_copy(
            src_ref=src,
            dst_ref=dst,
            send_sem=send_sem,
            recv_sem=recv_sem,
            device_id=place,
            device_id_type=MESH,
        )

    def occ_copy(slot, side, there):
        column = c if side == 0 else 1 - c
        return send(
            occ_in.at[OWN, c, keep_own] if slot == OWN else packed.at[slot - 1],
            occ_in.at[there, c, keep_own],
            occ_send.at[slot, side],
            occ_recv.at[there, side],
            row=rows_of[slot],
            col=column,
        )

    def pass_copy(slot, part):
        slab = occ_in.at[slot, :, part]
        return send(slab, slab, pass_send.at[slot], pass_recv.at[slot], rep=other)

    def half_copy(slot, there):
        return send(
            half_out.at[slot - 1],
            half_in.at[there],
            h_send.at[slot],
            h_recv.at[there],
            row=rows_of[slot],
        )

    def virt_copy(slot, there):
        slab = virt_all.at[c, r, wide_own]
        return send(slab, slab, v1_send.at[slot], v1_recv.at[there], row=rows_of[slot])

    def v2_copy(column):
        slab = virt_all.at[column, :, wide_own]
        return send(slab, slab, v2_send.at[0], v2_recv.at[0], col=1 - c)

    def v3_copy(part):
        slab = virt_all.at[:, :, part]
        return send(slab, slab, v3_send.at[0], v3_recv.at[0], rep=other)

    pl.semaphore_wait(barrier, rows * cols)

    sends = [(FAR, 0), (ACROSS, 0), (FAR, 1), (ACROSS, 1), (NEAR, 0), (NEAR, 1), (OWN, 1)]
    for slot, side in sends:
        occ_copy(slot, side, slot_there[slot]).start()
    virt_copy(NEAR, NEAR).start()
    virt_copy(ACROSS, mine).start()
    virt_copy(FAR, mine).start()

    loads[6].wait()
    span = bs * aux
    gap = lax.broadcasted_iota(jnp.int32, (bs, span), 1) - aux * lax.broadcasted_iota(
        jnp.int32, (bs, span), 0
    )
    order = jnp.concatenate([(gap == p).astype(F32).astype(BF16) for p in range(aux)], axis=0)
    tall = lax.broadcasted_iota(jnp.int32, (span, bs), 0)
    n_live = (lax.broadcasted_iota(jnp.int32, (span, bs), 1) < sizes_ref[r]).astype(F32)
    lit = [
        loaded[b * span : (b + 1) * span, :]
        * (n_live * (tall < aux * sizes_ref[b]).astype(F32)).astype(BF16)
        for b in range(blocks)
    ]
    for j in range(most):
        weights = pick(r, j)
        value = sum(lit[b] * weights[b].astype(BF16) for b in range(blocks))
        turned = jnp.dot(order, value, preferred_element_type=F32).astype(BF16)
        for p in range(aux):
            chosen[j * bs : (j + 1) * bs, p * bs : (p + 1) * bs] = turned[p * bs : (p + 1) * bs]

    for slot in (FAR, ACROSS, NEAR, OWN):
        for side in range(cols):
            if slot != OWN or side:
                occ_copy(slot, side, slot).wait_recv()
        pass_copy(slot, keep_own).start()
    def halfway(slot):
        pass_copy(slot, keep_other).wait_recv()
        left = jnp.concatenate(
            [
                jnp.concatenate([occ_in[slot, side, j] for side in range(cols)], axis=0)
                for j in range(most)
            ],
            axis=1,
        )
        return jnp.dot(left, chosen[...], preferred_element_type=F32).astype(BF16)

    for slot in (FAR, ACROSS, NEAR):
        half_out[slot - 1] = halfway(slot)
        half_copy(slot, slot_there[slot]).start()
    half_in[OWN] = halfway(OWN)

    virt_copy(NEAR, NEAR).wait_recv()

    virt_copy(ACROSS, ACROSS).wait_recv()
    virt_copy(ACROSS, FAR).wait_recv()
    v2_copy(c).start()
    v2_copy(1 - c).wait_recv()
    v3_copy(wide_own).start()
    v3_copy(wide_other).wait_recv()

    def second(slot):
        source = rows_of[slot]
        right = jnp.concatenate(
            [
                jnp.concatenate([virt_all[side, source, block] for side in range(cols)], axis=0)
                for block in range(blocks)
            ],
            axis=1,
        )
        if slot != OWN:
            half_copy(slot, slot).wait_recv()
        for p in range(aux):
            term = jnp.dot(
                half_in[slot, :, p * bs : (p + 1) * bs], right, preferred_element_type=F32
            )
            if slot == OWN:
                total[p] = term
            else:
                total[p] += term

    for slot in (OWN, NEAR, ACROSS, FAR):
        second(slot)
    for p in range(aux):
        out_ref[p] = total[p].astype(BF16)

    for slot, side in sends:
        occ_copy(slot, side, slot_there[slot]).wait_send()
    for slot in names:
        pass_copy(slot, keep_own).wait_send()
        if slot != OWN:
            half_copy(slot, slot_there[slot]).wait_send()
    virt_copy(NEAR, NEAR).wait_send()
    virt_copy(ACROSS, mine).wait_send()
    virt_copy(FAR, mine).wait_send()
    v2_copy(c).wait_send()
    v3_copy(wide_own).wait_send()


def weave_kernel(aux, tiles, bs, lead, in_ref, out_ref):
    mixed = aux * tiles
    span = mixed * lead
    to = lax.broadcasted_iota(jnp.int32, (span, span), 0)
    come = lax.broadcasted_iota(jnp.int32, (span, span), 1)
    low = mixed.bit_length() - 1
    weave = (
        (come == (to & (mixed - 1)) * lead + lax.shift_right_logical(to, low))
        .astype(F32)
        .astype(BF16)
    )
    for part in range(in_ref.shape[1] // lead):
        piece = slice(part * lead, (part + 1) * lead)
        value = jnp.concatenate(
            [in_ref[p, piece, t * bs : (t + 1) * bs] for t in range(tiles) for p in range(aux)],
            axis=0,
        )
        out_ref[part * span : (part + 1) * span, :] = jnp.dot(
            weave, value, preferred_element_type=F32
        ).astype(BF16)


def call_weave(value):
    aux, bs, wide = value.shape
    tiles = wide // bs
    steps = 2
    return pl.pallas_call(
        functools.partial(weave_kernel, aux, tiles, bs, 16),
        grid=(steps,),
        out_shape=jax.ShapeDtypeStruct((bs * tiles * aux, bs), BF16),
        in_specs=[pl.BlockSpec((aux, bs // steps, wide), lambda i: (0, i, 0))],
        out_specs=pl.BlockSpec((bs * tiles * aux // steps, bs), lambda i: (i, 0)),
        compiler_params=pltpu.CompilerParams(vmem_limit_bytes=60 * 1024 * 1024),
        name="weave",
    )(value)


def call_four(dims, operands):
    rows, cols, blocks, most, bs, chunk, aux = dims
    span = aux * bs
    vmem = pl.BlockSpec(memory_space=pltpu.VMEM)
    dma = pltpu.SemaphoreType.DMA
    one, slots = dma((1,)), dma((4,))
    return pl.pallas_call(
        functools.partial(kernel_four, dims),
        out_shape=jax.ShapeDtypeStruct((aux, bs, blocks * bs), BF16),
        in_specs=[pl.BlockSpec(memory_space=pl.ANY)] * 7,
        out_specs=vmem,
        scratch_shapes=[
            pltpu.VMEM((blocks, chunk, bs), F32),
            pltpu.VMEM((3, most // 2, chunk, bs), BF16),
            pltpu.VMEM((4, cols, most, chunk, bs), BF16),
            pltpu.VMEM((cols, rows, blocks, chunk, bs), BF16),
            pltpu.VMEM((most * bs, span), BF16),
            pltpu.VMEM((3, bs, span), BF16),
            pltpu.VMEM((4, bs, span), BF16),
            pltpu.VMEM((aux, bs, blocks * bs), F32),
            dma((4, cols)),
            dma((4, cols)),
            slots,
            slots,
            slots,
            slots,
            slots,
            slots,
            one,
            one,
            one,
            one,
            pltpu.VMEM((blocks * span, bs), BF16),
            pltpu.VMEM((chunk, blocks * bs), BF16),
            pltpu.VMEM((chunk, blocks * bs), BF16),
            pltpu.SMEM((blocks, blocks), jnp.int32),
            pltpu.SMEM((blocks, blocks), jnp.int32),
            pltpu.SMEM((blocks, blocks), jnp.int32),
            pltpu.SMEM((blocks,), jnp.int32),
            dma((7,)),
        ],
        compiler_params=pltpu.CompilerParams(
            collective_id=0, has_side_effects=True, vmem_limit_bytes=60 * 1024 * 1024
        ),
        name="contract",
    )(*operands)


def per_device(rows, cols, integrals, occupied, virtual, pair_mask, occ_mask, virt_mask, sizes):
    total_ao, aux, ao_local = integrals.shape
    blocks = sizes.shape[0]
    bs = total_ao // blocks
    most = max(blocks // 2, 1)
    chunk = occupied.shape[0]
    dims = (rows, cols, blocks, most, bs, chunk, aux)
    if rows == 4 and cols == 2 and most % 2 == 0 and blocks == rows:
        flat = integrals.reshape(total_ao * aux, ao_local)
        result = call_four(
            dims, (pair_mask, occ_mask, virt_mask, sizes, flat, occupied, virtual)
        )
        result = call_weave(result).reshape(bs, blocks, aux, bs).transpose(0, 2, 1, 3)
        return result.reshape(bs, aux, total_ao)
    smem = pl.BlockSpec(memory_space=pltpu.SMEM)
    vmem = pl.BlockSpec(memory_space=pltpu.VMEM)
    dma = pltpu.SemaphoreType.DMA
    result = pl.pallas_call(
        functools.partial(kernel, dims),
        out_shape=jax.ShapeDtypeStruct((bs, aux * total_ao), BF16),
        in_specs=[smem] * 4 + [vmem] * 3,
        out_specs=vmem,
        scratch_shapes=[
            pltpu.VMEM((blocks, chunk, bs), F32),
            pltpu.VMEM((rows, most // 2, chunk, bs), BF16),
            pltpu.VMEM((rows, cols, most, chunk, bs), BF16),
            pltpu.VMEM((cols, rows, blocks, chunk, bs), BF16),
            pltpu.VMEM((most * bs, aux * ao_local), BF16),
            pltpu.VMEM((rows, bs, aux * ao_local), BF16),
            pltpu.VMEM((rows, bs, aux * ao_local), BF16),
            pltpu.VMEM((aux, bs, total_ao), F32),
            dma((rows, cols)),
            dma((rows, cols)),
            dma((rows,)),
            dma((rows,)),
            dma((rows,)),
            dma((rows,)),
            dma((cols,)),
            dma((cols,)),
            dma((1,)),
            dma((1,)),
            dma((rows,)),
            dma((rows,)),
        ],
        compiler_params=pltpu.CompilerParams(
            collective_id=0, has_side_effects=True, vmem_limit_bytes=48 * 1024 * 1024
        ),
        name="contract",
    )(
        pair_mask,
        occ_mask,
        virt_mask,
        sizes,
        integrals.reshape(total_ao, aux * ao_local),
        occupied,
        virtual,
    )
    return result.reshape(bs, aux, total_ao)


def solution(mesh):
    in_specs = (
        P(None, ("grp", "col", "rep"), "row"),
        P(("grp", "row", "col"), None),
        P(("grp", "row", "col"), None),
        P(),
        P(),
        P(),
        P(),
    )
    out_specs = P("row", ("grp", "col", "rep"), None)
    return jax.shard_map(
        functools.partial(per_device, mesh.shape["row"], mesh.shape["col"]),
        mesh=mesh,
        in_specs=in_specs,
        out_specs=out_specs,
        check_vma=False,
    )
```

```python
import functools

import jax
import jax.numpy as jnp
from jax import lax
from jax.experimental import pallas as pl
from jax.experimental.pallas import tpu as pltpu
from jax.sharding import PartitionSpec as P

MESH = pl.DeviceIdType.MESH
F32 = jnp.float32
BF16 = jnp.bfloat16


def loop(count, body):
    if count <= 4:
        for step in range(count):
            body(step)
    else:
        lax.fori_loop(0, count, lambda step, _: (body(step), 0)[1], 0)


def kernel(
    dims,
    pair_ref,
    occ_mask_ref,
    virt_mask_ref,
    sizes_ref,
    tensor_ref,
    occ_ref,
    virt_ref,
    out_ref,
    masked,
    packed,
    occ_all,
    virt_all,
    chosen,
    half_out,
    half_in,
    total,
    occ_send,
    occ_recv,
    pass_send,
    pass_recv,
    v1_send,
    v1_recv,
    v2_send,
    v2_recv,
    v3_send,
    v3_recv,
    h_send,
    h_recv,
):
    rows, cols, blocks, most, bs, chunk, aux = dims
    r = lax.axis_index("row")
    c = lax.axis_index("col")
    rep = lax.axis_index("rep")
    other = 1 - rep
    keep = most // 2
    wide = blocks // 2
    keep_own, keep_other = pl.ds(rep * keep, keep), pl.ds(other * keep, keep)
    wide_own, wide_other = pl.ds(rep * wide, wide), pl.ds(other * wide, wide)

    def row_at(step):
        return lax.rem(r + step, rows)

    def row_from(step):
        return lax.rem(r + rows - step, rows)

    def col_at(step):
        return lax.rem(c + step, cols)

    def col_from(step):
        return lax.rem(c + cols - step, cols)

    barrier = pltpu.get_barrier_semaphore()

    def greet(step):
        pl.semaphore_signal(
            barrier,
            inc=1,
            device_id={"row": row_at(step // cols), "col": col_at(step % cols)},
            device_id_type=MESH,
        )

    if rows * cols <= 8:
        for step in range(1, rows * cols):
            greet(step)
    else:
        lax.fori_loop(1, rows * cols, lambda step, _: (greet(step), 0)[1], 0)
    pl.semaphore_signal(barrier, inc=1, device_id={"rep": other}, device_id_type=MESH)

    def pick(column, place):
        weights, seen = [], jnp.int32(0)
        for block in range(blocks):
            here = (pair_ref[block, column] != 0).astype(jnp.int32)
            weights.append((here * (seen == place).astype(jnp.int32)).astype(F32))
            seen = seen + here
        return weights

    lane = lax.broadcasted_iota(jnp.int32, (chunk, bs), 1)
    in_block = c * chunk + lax.broadcasted_iota(jnp.int32, (chunk, bs), 0)
    row_live = (in_block < sizes_ref[r]).astype(F32)

    for block in range(blocks):
        values = occ_ref[:, block * bs : (block + 1) * bs].astype(F32)
        live = (lane < sizes_ref[block]).astype(F32)
        weight = occ_mask_ref[r, block].astype(F32)
        masked[block] = values * (live * row_live * weight)

    def pack(step):
        for j in range(keep):
            weights = pick(row_at(step), rep * keep + j)
            packed[step, j] = sum(masked[b] * weights[b] for b in range(blocks)).astype(BF16)

    loop(rows, pack)
    occ_all[r, c, keep_own] = packed[0]
    for place in range(wide):
        block = rep * wide + place
        values = virt_ref[:, pl.ds(pl.multiple_of(block * bs, bs), bs)].astype(F32)
        live = (lane < sizes_ref[block]).astype(F32)
        weight = virt_mask_ref[r, block].astype(F32)
        virt_all[c, r, block] = (values * (live * row_live * weight)).astype(BF16)

    pl.semaphore_wait(barrier, rows * cols)

    def occ_copy(step, side, source_r, source_c):
        return pltpu.make_async_remote_copy(
            src_ref=packed.at[step],
            dst_ref=occ_all.at[source_r, source_c, keep_own],
            send_sem=occ_send.at[step, side],
            recv_sem=occ_recv.at[step, side],
            device_id={"row": row_at(step), "col": col_at(side)},
            device_id_type=MESH,
        )

    def send_occ(step):
        for side in range(cols):
            if isinstance(step, int) and step == 0 and side == 0:
                continue
            occ_copy(step, side, r, c).start()

    def send_v1(step):
        v1_copy(step, r).start()

    def v1_copy(step, source_r):
        return pltpu.make_async_remote_copy(
            src_ref=virt_all.at[c, source_r, wide_own],
            dst_ref=virt_all.at[c, source_r, wide_own],
            send_sem=v1_send.at[step],
            recv_sem=v1_recv.at[step],
            device_id={"row": row_at(step)},
            device_id_type=MESH,
        )

    def v2_copy(side, source_c):
        return pltpu.make_async_remote_copy(
            src_ref=virt_all.at[source_c, :, wide_own],
            dst_ref=virt_all.at[source_c, :, wide_own],
            send_sem=v2_send.at[side],
            recv_sem=v2_recv.at[side],
            device_id={"col": col_at(side)},
            device_id_type=MESH,
        )

    def v3_copy(part):
        return pltpu.make_async_remote_copy(
            src_ref=virt_all.at[:, :, part],
            dst_ref=virt_all.at[:, :, part],
            send_sem=v3_send.at[0],
            recv_sem=v3_recv.at[0],
            device_id={"rep": other},
            device_id_type=MESH,
        )

    def pass_copy(block, part):
        return pltpu.make_async_remote_copy(
            src_ref=occ_all.at[block, :, part],
            dst_ref=occ_all.at[block, :, part],
            send_sem=pass_send.at[block],
            recv_sem=pass_recv.at[block],
            device_id={"rep": other},
            device_id_type=MESH,
        )

    def half_copy(step):
        return pltpu.make_async_remote_copy(
            src_ref=half_out.at[step],
            dst_ref=half_in.at[step],
            send_sem=h_send.at[step],
            recv_sem=h_recv.at[step],
            device_id={"row": row_at(step)},
            device_id_type=MESH,
        )

    far = rows - 1
    loop(far, lambda step: send_occ(step + 1))
    send_occ(0)
    loop(far, lambda step: send_v1(step + 1))

    tall = lax.broadcasted_iota(jnp.int32, (bs, bs), 0)
    across = lax.broadcasted_iota(jnp.int32, (bs, bs), 1)
    n_live = (across < sizes_ref[r]).astype(F32)
    picks = [pick(r, j) for j in range(most)]
    for p in range(aux):
        span = slice(p * bs, (p + 1) * bs)
        for j in range(most):
            terms = []
            for b in range(blocks):
                live = n_live * (tall < sizes_ref[b]).astype(F32) * picks[j][b]
                terms.append(tensor_ref[b * bs : (b + 1) * bs, span].astype(F32) * live)
            chosen[j * bs : (j + 1) * bs, span] = sum(terms).astype(BF16)

    def hand_on(step):
        source = row_from(step)
        for side in range(cols):
            if isinstance(step, int) and step == 0 and side == 0:
                continue
            occ_copy(step, side, source, col_from(side)).wait_recv()
        pass_copy(source, keep_own).start()

    loop(far, lambda step: hand_on(step + 1))
    hand_on(0)

    def first(step):
        goal = row_from(step)
        pass_copy(goal, keep_other).wait_recv()
        left = jnp.concatenate(
            [
                jnp.concatenate([occ_all[goal, side, j] for side in range(cols)], axis=0)
                for j in range(most)
            ],
            axis=1,
        )
        back = (rows - step) % rows
        result = jnp.dot(left, chosen[...], preferred_element_type=F32).astype(BF16)
        if isinstance(step, int) and step == 0:
            half_in[0] = result
        else:
            half_out[back] = result
            half_copy(back).start()

    loop(far, lambda step: first(step + 1))
    first(0)

    loop(far, lambda step: v1_copy(step + 1, row_from(step + 1)).wait_recv())
    loop(cols - 1, lambda side: v2_copy(side + 1, c).start())
    loop(cols - 1, lambda side: v2_copy(side + 1, col_from(side + 1)).wait_recv())
    v3_copy(wide_own).start()
    v3_copy(wide_other).wait_recv()

    def second(step):
        source = row_from(step)
        right = jnp.concatenate(
            [
                jnp.concatenate([virt_all[side, source, block] for side in range(cols)], axis=0)
                for block in range(blocks)
            ],
            axis=1,
        )
        if not (isinstance(step, int) and step == 0):
            half_copy(step).wait_recv()
        for p in range(aux):
            term = jnp.dot(
                half_in[step, :, p * bs : (p + 1) * bs], right, preferred_element_type=F32
            )
            if isinstance(step, int) and step == 0:
                total[p] = term
            else:
                total[p] += term

    second(0)
    loop(far, lambda step: second(step + 1))
    span = blocks * bs
    for p in range(aux):
        out_ref[:, p * span : (p + 1) * span] = total[p].astype(BF16)

    def close_occ(step):
        for side in range(cols):
            if isinstance(step, int) and step == 0 and side == 0:
                continue
            occ_copy(step, side, r, c).wait_send()

    def close(step):
        close_occ(step + 1)
        v1_copy(step + 1, r).wait_send()
        half_copy(step + 1).wait_send()

    close_occ(0)
    loop(far, close)
    loop(rows, lambda block: pass_copy(block, keep_own).wait_send())
    loop(cols - 1, lambda side: v2_copy(side + 1, c).wait_send())
    v3_copy(wide_own).wait_send()


def kernel_four(
    dims,
    pair_hbm,
    occ_mask_hbm,
    virt_mask_hbm,
    sizes_hbm,
    tensor_hbm,
    occ_hbm,
    virt_hbm,
    out_ref,
    masked,
    packed,
    occ_in,
    virt_all,
    chosen,
    half_out,
    half_in,
    total,
    occ_send,
    occ_recv,
    pass_send,
    pass_recv,
    h_send,
    h_recv,
    v1_send,
    v1_recv,
    v2_send,
    v2_recv,
    v3_send,
    v3_recv,
    loaded,
    occ_ref,
    virt_ref,
    pair_ref,
    occ_mask_ref,
    virt_mask_ref,
    sizes_ref,
    load_sem,
):
    rows, cols, blocks, most, bs, chunk, aux = dims
    r = lax.axis_index("row")
    c = lax.axis_index("col")
    rep = lax.axis_index("rep")
    other = 1 - rep
    upper = r // 2
    near = r + 1 - 2 * (r % 2)
    across = 2 - upper
    far = 3 - 3 * upper
    outer_int = 1 - (r + upper) % 2
    keep = most // 2
    wide = blocks // 2
    keep_own = pl.ds(rep * keep, keep)
    keep_other = pl.ds(other * keep, keep)
    wide_own = pl.ds(rep * wide, wide)
    wide_other = pl.ds(other * wide, wide)
    OWN, NEAR, ACROSS, FAR = range(4)
    mine = ACROSS + outer_int
    rows_of = (r, near, across, far)
    names = (OWN, NEAR, ACROSS, FAR)
    slot_there = (OWN, NEAR, mine, mine)

    barrier = pltpu.get_barrier_semaphore()
    for step in range(1, rows * cols):
        pl.semaphore_signal(
            barrier,
            inc=1,
            device_id={"row": (r + step // cols) % rows, "col": (c + step) % cols},
            device_id_type=MESH,
        )
    pl.semaphore_signal(barrier, inc=1, device_id={"rep": other}, device_id_type=MESH)
    pairs = (
        (pair_hbm, pair_ref),
        (occ_mask_hbm, occ_mask_ref),
        (sizes_hbm, sizes_ref),
        (occ_hbm, occ_ref),
        (virt_mask_hbm, virt_mask_ref),
        (virt_hbm, virt_ref),
        (tensor_hbm, loaded),
    )
    loads = [
        pltpu.make_async_copy(src, dst, load_sem.at[i]) for i, (src, dst) in enumerate(pairs)
    ]
    for load in loads:
        load.start()
    for load in loads[:4]:
        load.wait()

    def pick(column, place):
        weights, seen = [], jnp.int32(0)
        for block in range(blocks):
            here = (pair_ref[block, column] != 0).astype(jnp.int32)
            weights.append((here * (seen == place).astype(jnp.int32)).astype(F32))
            seen = seen + here
        return weights

    lane = lax.broadcasted_iota(jnp.int32, (chunk, bs), 1)
    in_block = c * chunk + lax.broadcasted_iota(jnp.int32, (chunk, bs), 0)
    row_live = (in_block < sizes_ref[r]).astype(F32)
    for block in range(blocks):
        values = occ_ref[:, block * bs : (block + 1) * bs].astype(F32)
        live = (lane < sizes_ref[block]).astype(F32)
        weight = occ_mask_ref[r, block].astype(F32)
        masked[block] = values * (live * row_live * weight)

    def pack(goal):
        slabs = []
        for j in range(keep):
            weights = pick(goal, rep * keep + j)
            slabs.append(sum(masked[b] * weights[b] for b in range(blocks)).astype(BF16))
        return jnp.stack(slabs)

    for slot in (NEAR, ACROSS, FAR):
        packed[slot - 1] = pack(rows_of[slot])
    occ_in[OWN, c, keep_own] = pack(r)
    def send(src, dst, send_sem, recv_sem, **place):
        return pltpu.make_async_remote_copy(
            src_ref=src,
            dst_ref=dst,
            send_sem=send_sem,
            recv_sem=recv_sem,
            device_id=place,
            device_id_type=MESH,
        )

    def occ_copy(slot, side, there):
        column = c if side == 0 else 1 - c
        return send(
            occ_in.at[OWN, c, keep_own] if slot == OWN else packed.at[slot - 1],
            occ_in.at[there, c, keep_own],
            occ_send.at[slot, side],
            occ_recv.at[there, side],
            row=rows_of[slot],
            col=column,
        )

    def pass_copy(slot, part):
        slab = occ_in.at[slot, :, part]
        return send(slab, slab, pass_send.at[slot], pass_recv.at[slot], rep=other)

    def half_copy(slot, there):
        return send(
            half_out.at[slot - 1],
            half_in.at[there],
            h_send.at[slot],
            h_recv.at[there],
            row=rows_of[slot],
        )

    def virt_copy(slot, there):
        slab = virt_all.at[c, r, wide_own]
        return send(slab, slab, v1_send.at[slot], v1_recv.at[there], row=rows_of[slot])

    def v2_copy(slot, column):
        slab = virt_all.at[column, rows_of[slot], wide_own]
        return send(slab, slab, v2_send.at[slot], v2_recv.at[slot], col=1 - c)

    def v3_copy(slot, part):
        slab = virt_all.at[:, rows_of[slot], part]
        return send(slab, slab, v3_send.at[slot], v3_recv.at[slot], rep=other)

    pl.semaphore_wait(barrier, rows * cols)

    sends = [(FAR, 0), (ACROSS, 0), (FAR, 1), (ACROSS, 1), (NEAR, 0), (NEAR, 1), (OWN, 1)]
    for slot, side in sends:
        occ_copy(slot, side, slot_there[slot]).start()
    for load in loads[4:6]:
        load.wait()
    for place in range(wide):
        block = rep * wide + place
        values = virt_ref[:, pl.ds(pl.multiple_of(block * bs, bs), bs)].astype(F32)
        live = (lane < sizes_ref[block]).astype(F32)
        weight = virt_mask_ref[r, block].astype(F32)
        virt_all[c, r, block] = (values * (live * row_live * weight)).astype(BF16)
    virt_copy(NEAR, NEAR).start()
    virt_copy(ACROSS, mine).start()
    virt_copy(FAR, mine).start()

    loads[6].wait()
    span = bs * aux
    gap = lax.broadcasted_iota(jnp.int32, (bs, span), 1) - aux * lax.broadcasted_iota(
        jnp.int32, (bs, span), 0
    )
    order = jnp.concatenate([(gap == p).astype(F32).astype(BF16) for p in range(aux)], axis=0)
    tall = lax.broadcasted_iota(jnp.int32, (span, bs), 0)
    n_live = (lax.broadcasted_iota(jnp.int32, (span, bs), 1) < sizes_ref[r]).astype(F32)
    lit = [
        loaded[b * span : (b + 1) * span, :]
        * (n_live * (tall < aux * sizes_ref[b]).astype(F32)).astype(BF16)
        for b in range(blocks)
    ]
    for j in range(most):
        weights = pick(r, j)
        value = sum(lit[b] * weights[b].astype(BF16) for b in range(blocks))
        turned = jnp.dot(order, value, preferred_element_type=F32).astype(BF16)
        for p in range(aux):
            chosen[j * bs : (j + 1) * bs, p * bs : (p + 1) * bs] = turned[p * bs : (p + 1) * bs]

    for slot in (FAR, ACROSS, NEAR, OWN):
        for side in range(cols):
            if slot != OWN or side:
                occ_copy(slot, side, slot).wait_recv()
        pass_copy(slot, keep_own).start()
    def halfway(slot):
        pass_copy(slot, keep_other).wait_recv()
        left = jnp.concatenate(
            [
                jnp.concatenate([occ_in[slot, side, j] for side in range(cols)], axis=0)
                for j in range(most)
            ],
            axis=1,
        )
        return jnp.dot(left, chosen[...], preferred_element_type=F32).astype(BF16)

    for slot in (FAR, ACROSS, NEAR):
        half_out[slot - 1] = halfway(slot)
        half_copy(slot, slot_there[slot]).start()
    half_in[OWN] = halfway(OWN)

    v2_copy(OWN, c).start()
    for slot in (NEAR, ACROSS, FAR):
        virt_copy(slot, slot).wait_recv()
        v2_copy(slot, c).start()
    for slot in names:
        v2_copy(slot, 1 - c).wait_recv()
        v3_copy(slot, wide_own).start()

    def second(slot):
        source = rows_of[slot]
        v3_copy(slot, wide_other).wait_recv()
        right = jnp.concatenate(
            [
                jnp.concatenate([virt_all[side, source, block] for side in range(cols)], axis=0)
                for block in range(blocks)
            ],
            axis=1,
        )
        if slot != OWN:
            half_copy(slot, slot).wait_recv()
        for p in range(aux):
            term = jnp.dot(
                half_in[slot, :, p * bs : (p + 1) * bs], right, preferred_element_type=F32
            )
            if slot == OWN:
                total[p] = term
            else:
                total[p] += term

    for slot in (OWN, NEAR, ACROSS, FAR):
        second(slot)
    for p in range(aux):
        out_ref[p] = total[p].astype(BF16)

    for slot, side in sends:
        occ_copy(slot, side, slot_there[slot]).wait_send()
    for slot in names:
        pass_copy(slot, keep_own).wait_send()
        if slot != OWN:
            half_copy(slot, slot_there[slot]).wait_send()
    virt_copy(NEAR, NEAR).wait_send()
    virt_copy(ACROSS, mine).wait_send()
    virt_copy(FAR, mine).wait_send()
    for slot in names:
        v2_copy(slot, c).wait_send()
        v3_copy(slot, wide_own).wait_send()


def weave_kernel(aux, tiles, bs, lead, in_ref, out_ref):
    mixed = aux * tiles
    span = mixed * lead
    to = lax.broadcasted_iota(jnp.int32, (span, span), 0)
    come = lax.broadcasted_iota(jnp.int32, (span, span), 1)
    low = mixed.bit_length() - 1
    weave = (
        (come == (to & (mixed - 1)) * lead + lax.shift_right_logical(to, low))
        .astype(F32)
        .astype(BF16)
    )
    for part in range(in_ref.shape[1] // lead):
        piece = slice(part * lead, (part + 1) * lead)
        value = jnp.concatenate(
            [in_ref[p, piece, t * bs : (t + 1) * bs] for t in range(tiles) for p in range(aux)],
            axis=0,
        )
        out_ref[part * span : (part + 1) * span, :] = jnp.dot(
            weave, value, preferred_element_type=F32
        ).astype(BF16)


def call_weave(value):
    aux, bs, wide = value.shape
    tiles = wide // bs
    steps = 1
    return pl.pallas_call(
        functools.partial(weave_kernel, aux, tiles, bs, 16),
        grid=(steps,),
        out_shape=jax.ShapeDtypeStruct((bs * tiles * aux, bs), BF16),
        in_specs=[pl.BlockSpec((aux, bs // steps, wide), lambda i: (0, i, 0))],
        out_specs=pl.BlockSpec((bs * tiles * aux // steps, bs), lambda i: (i, 0)),
        compiler_params=pltpu.CompilerParams(vmem_limit_bytes=60 * 1024 * 1024),
        name="weave",
    )(value)


def call_four(dims, operands):
    rows, cols, blocks, most, bs, chunk, aux = dims
    span = aux * bs
    vmem = pl.BlockSpec(memory_space=pltpu.VMEM)
    dma = pltpu.SemaphoreType.DMA
    slots = dma((4,))
    return pl.pallas_call(
        functools.partial(kernel_four, dims),
        out_shape=jax.ShapeDtypeStruct((aux, bs, blocks * bs), BF16),
        in_specs=[pl.BlockSpec(memory_space=pl.ANY)] * 7,
        out_specs=vmem,
        scratch_shapes=[
            pltpu.VMEM((blocks, chunk, bs), F32),
            pltpu.VMEM((3, most // 2, chunk, bs), BF16),
            pltpu.VMEM((4, cols, most, chunk, bs), BF16),
            pltpu.VMEM((cols, rows, blocks, chunk, bs), BF16),
            pltpu.VMEM((most * bs, span), BF16),
            pltpu.VMEM((3, bs, span), BF16),
            pltpu.VMEM((4, bs, span), BF16),
            pltpu.VMEM((aux, bs, blocks * bs), F32),
            dma((4, cols)),
            dma((4, cols)),
            slots,
            slots,
            slots,
            slots,
            slots,
            slots,
            slots,
            slots,
            slots,
            slots,
            pltpu.VMEM((blocks * span, bs), BF16),
            pltpu.VMEM((chunk, blocks * bs), BF16),
            pltpu.VMEM((chunk, blocks * bs), BF16),
            pltpu.SMEM((blocks, blocks), jnp.int32),
            pltpu.SMEM((blocks, blocks), jnp.int32),
            pltpu.SMEM((blocks, blocks), jnp.int32),
            pltpu.SMEM((blocks,), jnp.int32),
            dma((7,)),
        ],
        compiler_params=pltpu.CompilerParams(
            collective_id=0, has_side_effects=True, vmem_limit_bytes=60 * 1024 * 1024
        ),
        name="contract",
    )(*operands)


def per_device(rows, cols, integrals, occupied, virtual, pair_mask, occ_mask, virt_mask, sizes):
    total_ao, aux, ao_local = integrals.shape
    blocks = sizes.shape[0]
    bs = total_ao // blocks
    most = max(blocks // 2, 1)
    chunk = occupied.shape[0]
    dims = (rows, cols, blocks, most, bs, chunk, aux)
    if rows == 4 and cols == 2 and most % 2 == 0 and blocks == rows:
        flat = integrals.reshape(total_ao * aux, ao_local)
        result = call_four(
            dims, (pair_mask, occ_mask, virt_mask, sizes, flat, occupied, virtual)
        )
        result = call_weave(result).reshape(bs, blocks, aux, bs).transpose(0, 2, 1, 3)
        return result.reshape(bs, aux, total_ao)
    smem = pl.BlockSpec(memory_space=pltpu.SMEM)
    vmem = pl.BlockSpec(memory_space=pltpu.VMEM)
    dma = pltpu.SemaphoreType.DMA
    result = pl.pallas_call(
        functools.partial(kernel, dims),
        out_shape=jax.ShapeDtypeStruct((bs, aux * total_ao), BF16),
        in_specs=[smem] * 4 + [vmem] * 3,
        out_specs=vmem,
        scratch_shapes=[
            pltpu.VMEM((blocks, chunk, bs), F32),
            pltpu.VMEM((rows, most // 2, chunk, bs), BF16),
            pltpu.VMEM((rows, cols, most, chunk, bs), BF16),
            pltpu.VMEM((cols, rows, blocks, chunk, bs), BF16),
            pltpu.VMEM((most * bs, aux * ao_local), BF16),
            pltpu.VMEM((rows, bs, aux * ao_local), BF16),
            pltpu.VMEM((rows, bs, aux * ao_local), BF16),
            pltpu.VMEM((aux, bs, total_ao), F32),
            dma((rows, cols)),
            dma((rows, cols)),
            dma((rows,)),
            dma((rows,)),
            dma((rows,)),
            dma((rows,)),
            dma((cols,)),
            dma((cols,)),
            dma((1,)),
            dma((1,)),
            dma((rows,)),
            dma((rows,)),
        ],
        compiler_params=pltpu.CompilerParams(
            collective_id=0, has_side_effects=True, vmem_limit_bytes=48 * 1024 * 1024
        ),
        name="contract",
    )(
        pair_mask,
        occ_mask,
        virt_mask,
        sizes,
        integrals.reshape(total_ao, aux * ao_local),
        occupied,
        virtual,
    )
    return result.reshape(bs, aux, total_ao)


def solution(mesh):
    in_specs = (
        P(None, ("grp", "col", "rep"), "row"),
        P(("grp", "row", "col"), None),
        P(("grp", "row", "col"), None),
        P(),
        P(),
        P(),
        P(),
    )
    out_specs = P("row", ("grp", "col", "rep"), None)
    return jax.shard_map(
        functools.partial(per_device, mesh.shape["row"], mesh.shape["col"]),
        mesh=mesh,
        in_specs=in_specs,
        out_specs=out_specs,
        check_vma=False,
    )
```
